256 devices in a mesh: row: 32 (over z, y), col: 8 (over x, core).
Axes of the slice: x: 4, y: 4, z: 8, core: 2. Of those that a mesh axis runs over, the one named last changes fastest.
Arguments:
- front_matrix: float32 [1, 32, 4, 8, 512, 512], P(None, 'row', None, 'col'), may hold values from -3 to 6, as said below
- block_map: int32 [64, 64], replicated, may hold values from 0 to 1, as said below
Outputs:
- factored: float32 [1, 32, 4, 8, 512, 512], P(None, 'row', None, 'col')
The draws below stay inside these ranges and needn't reach their ends.
Inputs may be any that keep to these rules, and one draw needn't show every extreme that they name: front_matrix holds a symmetric front in the layout of the first step; multiplied by block_map it is positive definite. block_map is symmetric and 1 on the diagonal; two profile blocks that are both marked nonzero against a third are marked nonzero against each other.
All inputs are finite; a program needn't handle non-finite values.
Results may differ from the reference program's by a relative error of at most 0.0001.
Values sent between devices are 32-bit elements; how exact they have to be, the bound alone decides.
No kernel may reach another device: no remote copies, remote signals or barrier semaphores. Data moves between devices by JAX's collectives and lax.ppermute only.
A program may use at most 128 MiB of HBM per device.

```python
import jax
import jax.numpy as jnp
from jax import lax

PW = 512
BS = 256
PANELS = 1
RBD = 1
GR = 32
GC = 8
NB = 32
CBD = 4
PB = 64


def draw_front_matrix(key, part):
    key = jax.random.fold_in(key, 7)
    order_all = NB * PW
    point_key, sign_key, shift_key = jax.random.split(key, 3)
    points = jax.random.uniform(point_key, (3, order_all), jnp.float32, 0.0, 4.0)
    signs = jnp.where(jax.random.bernoulli(sign_key, 0.5, (order_all,)), 1.0, -1.0).astype(jnp.float32)
    shifts = jax.random.uniform(shift_key, (order_all,), jnp.float32, 0.5, 1.5)
    distance = jnp.abs(points[0][:, None] - points[0][None, :])
    distance = distance + jnp.abs(points[1][:, None] - points[1][None, :])
    distance = distance + jnp.abs(points[2][:, None] - points[2][None, :])
    kernel = jnp.exp(-distance) * (signs[:, None] * signs[None, :])
    rows_index = lax.broadcasted_iota(jnp.int32, (order_all, order_all), 0)
    cols_index = lax.broadcasted_iota(jnp.int32, (order_all, order_all), 1)
    kernel = kernel + jnp.where(rows_index == cols_index, shifts[:, None], 0.0)
    symmetric = kernel
    return symmetric.reshape(RBD, GR, PW, CBD, GC, PW).transpose(0, 1, 3, 4, 2, 5)


def draw_block_map(key, part):
    key = jax.random.fold_in(key, 11)
    labels = jax.random.randint(key, (PB,), 0, 4, jnp.int32)
    return (labels[:, None] == labels[None, :]).astype(jnp.int32)


def setup_inputs(seed: int = 0) -> dict:
    key_list = jax.random.split(jax.random.key(seed), 3)
    return {
        "front_matrix": draw_front_matrix(jax.random.fold_in(key_list[2], 71), 0),
        "block_map": draw_block_map(jax.random.fold_in(key_list[2], 71), 0),
    }


HIGHEST_PRECISION = lax.Precision.HIGHEST

def reference(front_matrix, block_map):
    order_all = NB * PW
    dense_front = jnp.transpose(front_matrix, (0, 1, 4, 2, 3, 5)).reshape(order_all, order_all)
    weights = block_map.astype(jnp.float32)
    working = (dense_front.reshape(PB, BS, PB, BS) * weights[:, None, :, None]).reshape(order_all, order_all)
    columns = []
    for current in range(PANELS):
        lower_edge = current * PW
        upper_edge = lower_edge + PW
        pivot_factor = jnp.linalg.cholesky(working[lower_edge:upper_edge, lower_edge:upper_edge])
        below_rows = lax.linalg.triangular_solve(pivot_factor, working[upper_edge:, lower_edge:upper_edge].T, left_side=True, lower=True).T
        update = jnp.dot(below_rows.astype(jnp.float32), below_rows.T.astype(jnp.float32), precision=HIGHEST_PRECISION, preferred_element_type=jnp.float32)
        working = working.at[upper_edge:, upper_edge:].add(-update)
        columns.append(jnp.concatenate([jnp.zeros((lower_edge, PW), jnp.float32), pivot_factor, below_rows], axis=0))
    panel_edge = PANELS * PW
    trailing = working[:, panel_edge:]
    row_index = lax.broadcasted_iota(jnp.int32, trailing.shape, 0)
    trailing = jnp.where(row_index >= panel_edge, trailing, jnp.zeros_like(trailing))
    result = jnp.concatenate(columns + [trailing], axis=1)
    return result.reshape(RBD, GR, PW, CBD, GC, PW).transpose(0, 1, 3, 4, 2, 5)
```

```python
import jax
import jax.numpy as jnp
from jax import lax
from jax.experimental import pallas as pl
from jax.experimental.pallas import tpu as pltpu
from jax.sharding import PartitionSpec as P

BS = 256
N = 512
NB = 128
STEPS = N // NB
HIGHEST = lax.Precision.HIGHEST
BOTH = ("row", "col")
VMEM = pl.BlockSpec(memory_space=pltpu.VMEM)
SMEM = pl.BlockSpec(memory_space=pltpu.SMEM)


def dot_nn(a, b):
    return lax.dot_general(a, b, (((1,), (0,)), ((), ())), precision=HIGHEST, preferred_element_type=jnp.float32)


def dot_nt(a, b):
    return lax.dot_general(a, b, (((1,), (1,)), ((), ())), precision=HIGHEST, preferred_element_type=jnp.float32)


def spread_row(row):
    return jnp.broadcast_to(row, (8, NB))


def factor_block(d_ref, m_ref):
    row_ids = lax.broadcasted_iota(jnp.int32, (NB, NB), 0)
    col_ids = lax.broadcasted_iota(jnp.int32, (NB, NB), 1)
    m_ref[...] = jnp.where(row_ids == col_ids, 1.0, 0.0).astype(jnp.float32)
    for step in range(NB // 8):
        s = 8 * step
        d_rows = d_ref[s : s + 8, :]
        m_rows = m_ref[s : s + 8, :]
        cols = [spread_row(d_rows[:, s + j : s + j + 1]) for j in range(8)]
        a = {(i, j): spread_row(cols[j][i : i + 1, :]) for j in range(8) for i in range(j, 8)}
        low = {}
        inv = {}
        for j in range(8):
            r = lax.rsqrt(a[j, j])
            inv[j, j] = r
            for i in range(j + 1, 8):
                low[i, j] = a[i, j] * r
            for i in range(j + 1, 8):
                for k in range(j + 1, i + 1):
                    a[i, k] = a[i, k] - low[i, j] * low[k, j]
            for k in range(j):
                total = low[j, k] * inv[k, k]
                for t in range(k + 1, j):
                    total = total + low[j, t] * inv[t, k]
                inv[j, k] = -(r * total)

        def solve(rows):
            once = []
            for i in range(8):
                total = inv[i, 0] * rows[0]
                for k in range(1, i + 1):
                    total = total + inv[i, k] * rows[k]
                once.append(total)
            twice = []
            for k in range(8):
                total = inv[7, k] * once[7]
                for i in range(6, k - 1, -1):
                    total = total + inv[i, k] * once[i]
                twice.append(total)
            return once, twice

        _, d_twice = solve([spread_row(d_rows[k : k + 1, :]) for k in range(8)])
        m_once, m_twice = solve([spread_row(m_rows[k : k + 1, :]) for k in range(8)])
        for i in range(8):
            m_ref[s + i : s + i + 1, :] = m_once[i][0:1, :]
        for below in range(step + 1, NB // 8):
            t = 8 * below
            d_tile = d_ref[t : t + 8, :]
            d_sum = m_sum = 0.0
            for k in range(8):
                factor = spread_row(d_tile[:, s + k : s + k + 1])
                d_sum = d_sum + factor * d_twice[k]
                m_sum = m_sum + factor * m_twice[k]
            d_ref[t : t + 8, :] = d_tile - d_sum
            m_ref[t : t + 8, :] = m_ref[t : t + 8, :] - m_sum


def offset(b):
    return sum(N - NB * k for k in range(b))


def pivot_kernel(map_ref, a_ref, l_ref, inv_ref, w_ref, x_ref, d_ref, m_ref):
    coupled = map_ref[1, 0].astype(jnp.float32)
    w_ref[...] = a_ref[...]
    for b in range(2):
        start = offset(b) + BS - b * NB
        w_ref[start : offset(b + 1), :] = a_ref[start : offset(b + 1), :] * coupled
    row_ids = lax.broadcasted_iota(jnp.int32, (N, N), 0)
    col_ids = lax.broadcasted_iota(jnp.int32, (N, N), 1)
    x_ref[...] = jnp.where(row_ids == col_ids, 1.0, 0.0).astype(jnp.float32)
    for b in range(STEPS):
        o, e = b * NB, (b + 1) * NB
        panel = slice(offset(b), offset(b + 1))
        d_ref[...] = w_ref[offset(b) : offset(b) + NB, :]
        factor_block(d_ref, m_ref)
        m = m_ref[...]
        low = dot_nt(w_ref[panel, :], m)
        tri = lax.broadcasted_iota(jnp.int32, low.shape, 0) >= lax.broadcasted_iota(jnp.int32, low.shape, 1)
        l_ref[o:, o:e] = jnp.where(tri, low, 0.0)
        inv = dot_nn(m, x_ref[o:e, :e])
        inv_ref[o:e, :e] = inv
        if b:
            l_ref[:o, o:e] = jnp.zeros((o, NB), jnp.float32)
        if b < STEPS - 1:
            inv_ref[o:e, e:] = jnp.zeros((NB, N - e), jnp.float32)
            for k in range(b + 1, STEPS):
                rest = low[(k - b) * NB :]
                w_ref[offset(k) : offset(k + 1), :] -= dot_nt(rest, rest[:NB])
            x_ref[e:, :e] -= dot_nn(low[NB:], inv)


def pivot(block_map, packed):
    return pl.pallas_call(
        pivot_kernel,
        out_shape=(jax.ShapeDtypeStruct((N, N), jnp.float32),) * 2,
        in_specs=[SMEM, VMEM],
        out_specs=(VMEM, VMEM),
        scratch_shapes=[
            pltpu.VMEM((offset(STEPS), NB), jnp.float32),
            pltpu.VMEM((N, N), jnp.float32),
            pltpu.VMEM((NB, NB), jnp.float32),
            pltpu.VMEM((NB, NB), jnp.float32),
        ],
        name="pivot_cholesky",
    )(block_map, packed)


def weigh(block, w00, w01, w10, w11):
    rows = lax.broadcasted_iota(jnp.int32, block.shape, 0) < BS
    cols = lax.broadcasted_iota(jnp.int32, block.shape, 1) < BS
    return block * jnp.where(rows, jnp.where(cols, w00, w01), jnp.where(cols, w10, w11))


def update_kernel(place_ref, map_ref, front_ref, col_ref, row_ref, l_ref, inv_ref, out_ref, row_factor_ref):
    c = pl.program_id(0)
    p, q = place_ref[0], place_ref[1]
    j = c * 8 + q

    def weight(r, s):
        return map_ref[r, s].astype(jnp.float32)

    def weights(r, s):
        return [weight(2 * r + a, 2 * s + b) for a in range(2) for b in range(2)]

    @pl.when(c == 0)
    def _():
        row_factor_ref[...] = dot_nt(weigh(row_ref[...], *weights(p, 0)), inv_ref[...])

    @pl.when(p > 0)
    def _():
        @pl.when(j > 0)
        def _():
            col_factor = dot_nt(weigh(col_ref[0], *weights(j, 0)), inv_ref[...])
            front = weigh(front_ref[0], *weights(p, j))
            out_ref[0] = front - dot_nt(row_factor_ref[...], col_factor)

        @pl.when(j == 0)
        def _():
            out_ref[0] = row_factor_ref[...]

    @pl.when(p == 0)
    def _():
        @pl.when(j > 0)
        def _():
            out_ref[0] = jnp.zeros((N, N), jnp.float32)

        @pl.when(j == 0)
        def _():
            out_ref[0] = l_ref[...]


def update(place, block_map, front, cols, rows, low, inv):
    count = front.shape[0]
    tile = pl.BlockSpec((1, N, N), lambda c: (c, 0, 0))
    whole = pl.BlockSpec((N, N), lambda c: (0, 0))
    return pl.pallas_call(
        update_kernel,
        grid=(count,),
        out_shape=jax.ShapeDtypeStruct((count, N, N), jnp.float32),
        in_specs=[SMEM, SMEM, tile, tile, whole, whole, whole],
        out_specs=tile,
        scratch_shapes=[pltpu.VMEM((N, N), jnp.float32)],
        name="schur_update",
    )(place, block_map, front, cols, rows, low, inv)


def device(z, y, x, core):
    return ((z % 8 * 4 + y % 4) * 4 + x % 4) * 2 + core


def tree(value, z, y, x, core):
    rounds = [
        [([(device(0, 0, 0, 0), device(0, 0, d, 0))], x == d) for d in (1, 3, 2)],
        [([(device(0, 0, i, 0), device(0, d, i, 0)) for i in range(4)], y == d) for d in (1, 3, 2)],
        [([(device(0, j, i, 0), device(4, j, i, 0)) for j in range(4) for i in range(4)], z == 4)],
        [
            ([(device(k, j, i, 0), device(k + d, j, i, 0)) for k in (0, 4) for j in range(4) for i in range(4)], z % 4 == d % 4)
            for d in (1, 7, 2)
        ],
        [([(device(k, j, i, 0), device(k, j, i, 1)) for k in range(8) for j in range(4) for i in range(4)], core == 1)],
    ]
    for sends in rounds:
        arrived = [(hit, lax.ppermute(value, BOTH, pairs)) for pairs, hit in sends]
        for hit, got in arrived:
            value = jnp.where(hit, got, value)
    return value


def body(front_matrix, block_map):
    front = front_matrix[0, 0, :, 0]
    p = lax.axis_index("row")
    q = lax.axis_index("col")
    head = front[0]

    packed = jnp.concatenate([head[b * NB :, b * NB : (b + 1) * NB] for b in range(STEPS)], axis=0)
    packed = tree(packed, p // 4, p % 4, q // 2, q % 2)

    chunk = N // 8
    piece = jnp.zeros((chunk, N), jnp.float32)
    for t in range(8):
        pairs = [(s * 8, (s // 8 * 8 + t) * 8 + s % 8) for s in range(32)]
        got = lax.ppermute(head[t * chunk : (t + 1) * chunk], BOTH, pairs)
        piece = jnp.where(p % 8 == t, got, piece)
    cols = lax.all_gather(piece, "row").reshape(4, N, N)

    row = head
    arrived = [(x, lax.ppermute(head, "col", [(0, 2 * x)])) for x in (1, 3, 2)]
    for x, got in arrived:
        row = jnp.where(q == 2 * x, got, row)
    other = lax.ppermute(row, "col", [(2 * x, 2 * x + 1) for x in range(4)])
    row = jnp.where(q % 2 == 1, other, row)

    low, inv = pivot(block_map, packed)
    place = jnp.stack([p, q]).astype(jnp.int32)
    out = update(place, block_map, front, cols, row, low, inv)
    return out.reshape(front_matrix.shape)


def solution(mesh):
    return jax.shard_map(
        body,
        mesh=mesh,
        in_specs=(P(None, "row", None, "col", None, None), P()),
        out_specs=P(None, "row", None, "col", None, None),
        check_vma=False,
    )
```

```python
import jax
import jax.numpy as jnp
from jax import lax
from jax.experimental import pallas as pl
from jax.experimental.pallas import tpu as pltpu
from jax.sharding import PartitionSpec as P

BS = 256
N = 512
NB = 128
STEPS = N // NB
SPLIT = 16
HIGHEST = lax.Precision.HIGHEST
BOTH = ("row", "col")
VMEM = pl.BlockSpec(memory_space=pltpu.VMEM)
SMEM = pl.BlockSpec(memory_space=pltpu.SMEM)


def dot_nn(a, b):
    return lax.dot_general(a, b, (((1,), (0,)), ((), ())), precision=HIGHEST, preferred_element_type=jnp.float32)


def dot_nt(a, b):
    return lax.dot_general(a, b, (((1,), (1,)), ((), ())), precision=HIGHEST, preferred_element_type=jnp.float32)


def spread_row(row):
    return jnp.broadcast_to(row, (8, NB))


def factor_block(d_ref, m_ref):
    row_ids = lax.broadcasted_iota(jnp.int32, (NB, NB), 0)
    col_ids = lax.broadcasted_iota(jnp.int32, (NB, NB), 1)
    m_ref[...] = jnp.where(row_ids == col_ids, 1.0, 0.0).astype(jnp.float32)
    for step in range(NB // 8):
        s = 8 * step
        d_rows = d_ref[s : s + 8, :]
        m_rows = m_ref[s : s + 8, :]
        cols = [spread_row(d_rows[:, s + j : s + j + 1]) for j in range(8)]
        a = {(i, j): spread_row(cols[j][i : i + 1, :]) for j in range(8) for i in range(j, 8)}
        low = {}
        inv = {}
        for j in range(8):
            r = lax.rsqrt(a[j, j])
            inv[j, j] = r
            for i in range(j + 1, 8):
                low[i, j] = a[i, j] * r
            for i in range(j + 1, 8):
                for k in range(j + 1, i + 1):
                    a[i, k] = a[i, k] - low[i, j] * low[k, j]
            for k in range(j):
                total = low[j, k] * inv[k, k]
                for t in range(k + 1, j):
                    total = total + low[j, t] * inv[t, k]
                inv[j, k] = -(r * total)

        def solve(rows):
            once = []
            for i in range(8):
                total = inv[i, 0] * rows[0]
                for k in range(1, i + 1):
                    total = total + inv[i, k] * rows[k]
                once.append(total)
            twice = []
            for k in range(8):
                total = inv[7, k] * once[7]
                for i in range(6, k - 1, -1):
                    total = total + inv[i, k] * once[i]
                twice.append(total)
            return once, twice

        _, d_twice = solve([spread_row(d_rows[k : k + 1, :]) for k in range(8)])
        m_once, m_twice = solve([spread_row(m_rows[k : k + 1, :]) for k in range(8)])
        for i in range(8):
            m_ref[s + i : s + i + 1, :] = m_once[i][0:1, :]
        for below in range(step + 1, NB // 8):
            t = 8 * below
            d_tile = d_ref[t : t + 8, :]
            d_sum = m_sum = 0.0
            for k in range(8):
                factor = spread_row(d_tile[:, s + k : s + k + 1])
                d_sum = d_sum + factor * d_twice[k]
                m_sum = m_sum + factor * m_twice[k]
            d_ref[t : t + 8, :] = d_tile - d_sum
            m_ref[t : t + 8, :] = m_ref[t : t + 8, :] - m_sum


def offset(b):
    return sum(N - NB * k for k in range(b))


def pivot_kernel(map_ref, a_ref, l_ref, inv_ref, w_ref, x_ref, d_ref, m_ref):
    coupled = map_ref[1, 0].astype(jnp.float32)
    w_ref[...] = a_ref[...]
    for b in range(2):
        start = offset(b) + BS - b * NB
        w_ref[start : offset(b + 1), :] = a_ref[start : offset(b + 1), :] * coupled
    row_ids = lax.broadcasted_iota(jnp.int32, (N, N), 0)
    col_ids = lax.broadcasted_iota(jnp.int32, (N, N), 1)
    x_ref[...] = jnp.where(row_ids == col_ids, 1.0, 0.0).astype(jnp.float32)
    for b in range(STEPS):
        o, e = b * NB, (b + 1) * NB
        panel = slice(offset(b), offset(b + 1))
        d_ref[...] = w_ref[offset(b) : offset(b) + NB, :]
        factor_block(d_ref, m_ref)
        m = m_ref[...]
        low = dot_nt(w_ref[panel, :], m)
        tri = lax.broadcasted_iota(jnp.int32, low.shape, 0) >= lax.broadcasted_iota(jnp.int32, low.shape, 1)
        l_ref[o:, o:e] = jnp.where(tri, low, 0.0)
        inv = dot_nn(m, x_ref[o:e, :e])
        inv_ref[o:e, :e] = inv
        if b:
            l_ref[:o, o:e] = jnp.zeros((o, NB), jnp.float32)
        if b < STEPS - 1:
            inv_ref[o:e, e:] = jnp.zeros((NB, N - e), jnp.float32)
            for k in range(b + 1, STEPS):
                rest = low[(k - b) * NB :]
                w_ref[offset(k) : offset(k + 1), :] -= dot_nt(rest, rest[:NB])
            x_ref[e:, :e] -= dot_nn(low[NB:], inv)


def pivot(block_map, packed):
    return pl.pallas_call(
        pivot_kernel,
        out_shape=(jax.ShapeDtypeStruct((N, N), jnp.float32),) * 2,
        in_specs=[SMEM, VMEM],
        out_specs=(VMEM, VMEM),
        scratch_shapes=[
            pltpu.VMEM((offset(STEPS), NB), jnp.float32),
            pltpu.VMEM((N, N), jnp.float32),
            pltpu.VMEM((NB, NB), jnp.float32),
            pltpu.VMEM((NB, NB), jnp.float32),
        ],
        name="pivot_cholesky",
    )(block_map, packed)


def weigh(block, w00, w01, w10, w11):
    rows = lax.broadcasted_iota(jnp.int32, block.shape, 0) < BS
    cols = lax.broadcasted_iota(jnp.int32, block.shape, 1) < BS
    return block * jnp.where(rows, jnp.where(cols, w00, w01), jnp.where(cols, w10, w11))


def update_kernel(place_ref, map_ref, front_ref, upper_ref, lower_ref, row_ref, l_ref, inv_ref, out_ref, row_factor_ref, col_ref):
    c = pl.program_id(0)
    p, q = place_ref[0], place_ref[1]
    j = c * 8 + q

    def weight(r, s):
        return map_ref[r, s].astype(jnp.float32)

    def weights(r, s):
        return [weight(2 * r + a, 2 * s + b) for a in range(2) for b in range(2)]

    @pl.when(c == 0)
    def _():
        row_factor_ref[...] = dot_nt(weigh(row_ref[...], *weights(p, 0)), inv_ref[...])

    @pl.when(p > 0)
    def _():
        @pl.when(j > 0)
        def _():
            for t in range(8):
                start = t * (N // 8)
                col_ref[start : start + SPLIT, :] = upper_ref[0, t // 4, t % 4]
                col_ref[start + SPLIT : start + N // 8, :] = lower_ref[t % 4, 0, t // 4]
            col_factor = dot_nt(weigh(col_ref[...], *weights(j, 0)), inv_ref[...])
            front = weigh(front_ref[0], *weights(p, j))
            out_ref[0] = front - dot_nt(row_factor_ref[...], col_factor)

        @pl.when(j == 0)
        def _():
            out_ref[0] = row_factor_ref[...]

    @pl.when(p == 0)
    def _():
        @pl.when(j > 0)
        def _():
            out_ref[0] = jnp.zeros((N, N), jnp.float32)

        @pl.when(j == 0)
        def _():
            out_ref[0] = l_ref[...]


def update(place, block_map, front, upper, lower, rows, low, inv):
    count = front.shape[0]
    tile = pl.BlockSpec((1, N, N), lambda c: (c, 0, 0))
    whole = pl.BlockSpec((N, N), lambda c: (0, 0))
    return pl.pallas_call(
        update_kernel,
        grid=(count,),
        out_shape=jax.ShapeDtypeStruct((count, N, N), jnp.float32),
        in_specs=[
            SMEM,
            SMEM,
            tile,
            pl.BlockSpec((1, 2, 4, SPLIT, N), lambda c: (c, 0, 0, 0, 0)),
            pl.BlockSpec((4, 1, 2, N // 8 - SPLIT, N), lambda c: (0, c, 0, 0, 0)),
            whole,
            whole,
            whole,
        ],
        out_specs=tile,
        scratch_shapes=[pltpu.VMEM((N, N), jnp.float32), pltpu.VMEM((N, N), jnp.float32)],
        name="schur_update",
    )(place, block_map, front, upper, lower, rows, low, inv)


def device(z, y, x, core):
    return ((z % 8 * 4 + y % 4) * 4 + x % 4) * 2 + core


Y_GROUPS = [[z * 4 + y for y in range(4)] for z in range(8)]
Z_GROUPS = [[z * 4 + y for z in range(8)] for y in range(4)]


def gather(value, axis, size, groups=None):
    return lax.all_to_all(jnp.broadcast_to(value, (size, *value.shape)), axis, 0, 0, axis_index_groups=groups)


def plane_tree(value, z, y):
    lanes = [(i, k) for i in range(4) for k in range(2)]
    rounds = [
        [([(device(0, 0, i, k), device(0, d, i, k)) for i, k in lanes], y == d) for d in (1, 3, 2)],
        [([(device(0, j, i, k), device(4, j, i, k)) for j in range(4) for i, k in lanes], z == 4)],
        [
            ([(device(s, j, i, k), device(s + d, j, i, k)) for s in (0, 4) for j in range(4) for i, k in lanes], z % 4 == d % 4)
            for d in (1, 7, 2)
        ],
    ]
    for sends in rounds:
        arrived = [(hit, lax.ppermute(value, BOTH, pairs)) for pairs, hit in sends]
        for hit, got in arrived:
            value = jnp.where(hit, got, value)
    return value


def body(front_matrix, block_map):
    front = front_matrix[0, 0, :, 0]
    p = lax.axis_index("row")
    q = lax.axis_index("col")
    head = front[0]

    packed = jnp.concatenate([head[b * NB :, b * NB : (b + 1) * NB] for b in range(STEPS)], axis=0)
    share = lax.all_to_all(packed.reshape(8, -1, NB), "col", 0, 0)[0]
    share = plane_tree(share, p // 4, p % 4)
    packed = gather(share, "col", 8).reshape(-1, NB)

    chunk = N // 8
    piece = jnp.zeros((chunk, N), jnp.float32)
    for t in range(8):
        pairs = [(s * 8, (s // 8 * 8 + t) * 8 + s % 8) for s in range(32)]
        got = lax.ppermute(head[t * chunk : (t + 1) * chunk], BOTH, pairs)
        piece = jnp.where(p % 8 == t, got, piece)
    upper, lower = piece[:SPLIT], piece[SPLIT:]
    lower = gather(lower, "row", 8, Z_GROUPS)
    upper = gather(upper, "row", 4, Y_GROUPS)
    lower = gather(lower, "row", 4, Y_GROUPS).reshape(4, 4, 2, chunk - SPLIT, N)
    upper = gather(upper, "row", 8, Z_GROUPS).reshape(4, 2, 4, SPLIT, N)

    row = head
    arrived = [(x, lax.ppermute(head, "col", [(0, 2 * x)])) for x in (1, 3, 2)]
    for x, got in arrived:
        row = jnp.where(q == 2 * x, got, row)
    other = lax.ppermute(row, "col", [(2 * x, 2 * x + 1) for x in range(4)])
    row = jnp.where(q % 2 == 1, other, row)

    low, inv = pivot(block_map, packed)
    place = jnp.stack([p, q]).astype(jnp.int32)
    out = update(place, block_map, front, upper, lower, row, low, inv)
    return out.reshape(front_matrix.shape)


def solution(mesh):
    return jax.shard_map(
        body,
        mesh=mesh,
        in_specs=(P(None, "row", None, "col", None, None), P()),
        out_specs=P(None, "row", None, "col", None, None),
        check_vma=False,
    )
```

```python
import functools

import jax
import jax.numpy as jnp
from jax import lax
from jax.experimental import pallas as pl
from jax.experimental.pallas import tpu as pltpu
from jax.sharding import PartitionSpec as P

BS = 256
N = 512
NB = 128
CHUNK = N // 8
HIGHEST = lax.Precision.HIGHEST
BOTH = ("row", "col")
VMEM = pl.BlockSpec(memory_space=pltpu.VMEM)
SMEM = pl.BlockSpec(memory_space=pltpu.SMEM)


def dot_nn(a, b):
    return lax.dot_general(a, b, (((1,), (0,)), ((), ())), precision=HIGHEST, preferred_element_type=jnp.float32)


def dot_nt(a, b):
    return lax.dot_general(a, b, (((1,), (1,)), ((), ())), precision=HIGHEST, preferred_element_type=jnp.float32)


def spread(row):
    return jnp.broadcast_to(row, (8, NB))


def factor_blocks(d_refs, m_refs):
    sub = lax.broadcasted_iota(jnp.int32, (8, NB), 0)
    lane = lax.broadcasted_iota(jnp.int32, (8, NB), 1)
    for first in range(0, NB, 32):
        tiles_of = [[d_ref[first + 8 * t : first + 8 * t + 8, :] for t in range(4)] for d_ref in d_refs]
        for step in range(4):
            s = first + 8 * step
            here = (lane >= s) & (lane < s + 8)
            state = []
            for tiles in tiles_of:
                cols = [spread(tiles[step][:, s + k : s + k + 1]) for k in range(8)]
                rows = jnp.where(here, jnp.where(lane == sub + s, 1.0, 0.0), tiles[step])
                state.append([cols, rows, jnp.ones_like(rows), rows])
            for j in range(8):
                own = sub == j
                for one in state:
                    cols, rows, diag, kept = one
                    d = cols[j][j : j + 1, :]
                    diag = jnp.where(own, spread(d), diag)
                    factor = jnp.where(own, 0.0, cols[j] * spread(1.0 / d))
                    for k in range(j + 1, 8):
                        cols[k] = cols[k] - factor * spread(cols[k][j : j + 1, :])
                    pivot_row = spread(rows[j : j + 1, :])
                    one[1:] = rows - factor * pivot_row, diag, jnp.where(own, pivot_row, kept)
            for tiles, m_ref, (_, rows, diag, kept) in zip(tiles_of, m_refs, state):
                m_ref[s : s + 8, :] = jnp.where(lane < s + 8, kept * lax.rsqrt(diag), 0.0)
                tiles[step] = rows / diag
                solved = [spread(tiles[step][k : k + 1, :]) for k in range(8)]
                for t in [*range(step + 1, 4), *range(step)]:
                    old = tiles[t]
                    terms = [spread(old[:, s + k : s + k + 1]) * solved[k] for k in range(8)]
                    while len(terms) > 1:
                        terms = [a + b for a, b in zip(terms[::2], terms[1::2])]
                    tiles[t] = jnp.where(here, 0.0, old) - terms[0]
        if first + 32 < NB:
            for tiles, d_ref in zip(tiles_of, d_refs):
                below = d_ref[first + 32 :, :]
                above = [jnp.zeros((first, NB), jnp.float32)] if first else []
                under = [jnp.zeros((NB - first - 32, NB), jnp.float32)]
                column = lax.broadcasted_iota(jnp.int32, below.shape, 1)
                inside = (column >= first) & (column < first + 32)
                product = dot_nn(below, jnp.concatenate(above + tiles + under, axis=0))
                d_ref[first + 32 :, :] = jnp.where(inside, 0.0, below) - product


def panels(groups):
    out, at = [], 0
    for b in range(N // groups // NB):
        for g in range(groups):
            height = N // groups - b * NB
            out.append((g, b, at, height))
            at += height
    return out


def packed_rows(groups):
    return sum(height for _, _, _, height in panels(groups))


def pivot_kernel(groups, place_ref, *refs):
    share_refs, (l_ref, inv_ref, w_ref, x_ref, d_ref, m_ref) = refs[:4], refs[4:]
    n = N // groups
    share = packed_rows(groups) // 4
    x = place_ref[1] // 2
    for step, ref in zip((0, 1, 3, 2), share_refs):
        w_ref[pl.ds(pl.multiple_of(lax.rem(x + step, 4) * share, 8), share), :] = ref[...]
    starts = {(g, b): (at, height) for g, b, at, height in panels(groups)}
    row_ids = lax.broadcasted_iota(jnp.int32, (n, n), 0)
    col_ids = lax.broadcasted_iota(jnp.int32, (n, n), 1)
    for g in range(groups):
        x_ref[g] = jnp.where(row_ids == col_ids, 1.0, 0.0).astype(jnp.float32)
    for b in range(n // NB):
        o, e = b * NB, (b + 1) * NB
        for g in range(groups):
            d_ref[g] = w_ref[pl.ds(starts[g, b][0], NB), :]
        factor_blocks([d_ref.at[g] for g in range(groups)], [m_ref.at[g] for g in range(groups)])
        for g in range(groups):
            at, height = starts[g, b]
            m = m_ref[g]
            low = dot_nt(w_ref[at : at + height, :], m)
            if e < n:
                for k in range(b + 1, n // NB):
                    rest = low[(k - b) * NB :]
                    to, rows = starts[g, k]
                    w_ref[to : to + rows, :] -= dot_nt(rest, rest[:NB])
            tri = lax.broadcasted_iota(jnp.int32, low.shape, 0) >= lax.broadcasted_iota(jnp.int32, low.shape, 1)
            l_ref[g, o:, o:e] = jnp.where(tri, low, 0.0)
            inv = dot_nn(m, x_ref[g, o:e, :e])
            inv_ref[g, o:e, :e] = inv
            if b:
                l_ref[g, :o, o:e] = jnp.zeros((o, NB), jnp.float32)
            if e < n:
                inv_ref[g, o:e, e:] = jnp.zeros((NB, n - e), jnp.float32)
                x_ref[g, e:, :e] -= dot_nn(low[NB:], inv)


def pivot(groups, place, shares):
    n = N // groups
    return pl.pallas_call(
        functools.partial(pivot_kernel, groups),
        out_shape=(jax.ShapeDtypeStruct((groups, n, n), jnp.float32),) * 2,
        in_specs=[SMEM] + [VMEM] * 4,
        out_specs=(VMEM, VMEM),
        scratch_shapes=[
            pltpu.VMEM((packed_rows(groups), NB), jnp.float32),
            pltpu.VMEM((groups, n, n), jnp.float32),
            pltpu.VMEM((groups, NB, NB), jnp.float32),
            pltpu.VMEM((groups, NB, NB), jnp.float32),
        ],
        name="pivot_cholesky",
    )(place, *shares)


def prepare_kernel(groups, place_ref, map_ref, head_ref, *out_refs):
    share_refs, chunk_refs, panel_ref = out_refs[:4], out_refs[4:12], out_refs[12]
    p = place_ref[0]
    n = N // groups
    for a in range(2):
        rows = slice(a * BS, (a + 1) * BS)
        panel = head_ref[0, rows, :n] * map_ref[2 * p + a, 0].astype(jnp.float32)
        if groups == 2:
            panel = panel + head_ref[0, rows, n:] * map_ref[2 * p + a, 1].astype(jnp.float32)
        panel_ref[rows, :] = panel
        for t in range(4):
            chunk_refs[4 * a + t][...] = panel[t * CHUNK : (t + 1) * CHUNK]
    lower = []
    for g, b, _, height in panels(groups):
        first = g * n + b * NB
        lower.append(head_ref[0, first : first + height, first : first + NB])
    lower = jnp.concatenate(lower, axis=0)
    share = packed_rows(groups) // 4
    for x in range(4):
        share_refs[x][...] = lower[x * share : (x + 1) * share]


def prepare(groups, place, block_map, front):
    n = N // groups
    shapes = [(packed_rows(groups) // 4, NB)] * 4 + [(CHUNK, n)] * 8 + [(N, n)]
    return pl.pallas_call(
        functools.partial(prepare_kernel, groups),
        grid=(1,),
        out_shape=tuple(jax.ShapeDtypeStruct(s, jnp.float32) for s in shapes),
        in_specs=[SMEM, SMEM, pl.BlockSpec((1, N, N), lambda i: (0, 0, 0))],
        out_specs=tuple(pl.BlockSpec(s, lambda i: (0, 0)) for s in shapes),
        name="prepare",
    )(place, block_map, front)


def update_kernel(groups, place_ref, map_ref, front_ref, col_ref, row_ref, l_ref, inv_ref, out_ref, row_factor_ref):
    c = pl.program_id(0)
    p, q = place_ref[0], place_ref[1]
    j = c * 8 + q
    n = N // groups

    def marked(r, s):
        return map_ref[r, s] != 0

    def in_panel(r):
        return marked(r, 0) | marked(r, 1)

    def inverse(r):
        return inv_ref[map_ref[r, 1]] if groups == 2 else inv_ref[0]

    @pl.when(c == 0)
    def _():
        for a in range(2):
            rows = slice(a * BS, (a + 1) * BS)
            row_factor_ref[rows, :] = dot_nt(row_ref[rows, :], inverse(2 * p + a))

    @pl.when((p > 0) & (j > 0))
    def _():
        for b in range(2):
            s = 2 * j + b
            cols = slice(b * BS, (b + 1) * BS)
            touched = [marked(2 * p + a, s) & in_panel(s) for a in range(2)]

            @pl.when(touched[0] | touched[1])
            def _():
                block = jnp.concatenate([col_ref[t, 0, b] for t in range(4)], axis=0)
                factor = dot_nt(block, inverse(s))
                for a in range(2):

                    @pl.when(touched[a])
                    def _():
                        rows = slice(a * BS, (a + 1) * BS)
                        out_ref[0, rows, cols] = front_ref[0, rows, cols] - dot_nt(row_factor_ref[rows, :], factor)

            for a in range(2):

                @pl.when(jnp.logical_not(touched[a]))
                def _():
                    rows = slice(a * BS, (a + 1) * BS)
                    weight = map_ref[2 * p + a, s].astype(jnp.float32)
                    out_ref[0, rows, cols] = front_ref[0, rows, cols] * weight

    @pl.when((p > 0) & (j == 0))
    def _():
        for a in range(2):
            rows = slice(a * BS, (a + 1) * BS)
            if groups == 1:
                out_ref[0, rows, :] = row_factor_ref[rows, :]
            else:
                for b in range(2):
                    weight = map_ref[2 * p + a, b].astype(jnp.float32)
                    out_ref[0, rows, b * BS : (b + 1) * BS] = row_factor_ref[rows, :] * weight

    @pl.when((p == 0) & (j > 0))
    def _():
        out_ref[0] = jnp.zeros((N, N), jnp.float32)

    @pl.when((p == 0) & (j == 0))
    def _():
        out_ref[0] = jnp.zeros((N, N), jnp.float32)
        for g in range(groups):
            out_ref[0, g * n : (g + 1) * n, g * n : (g + 1) * n] = l_ref[g]


def update(groups, place, block_map, front, cols, rows, low, inv):
    n = N // groups
    tile = pl.BlockSpec((1, N, N), lambda c: (c, 0, 0))
    square = pl.BlockSpec((groups, n, n), lambda c: (0, 0, 0))
    return pl.pallas_call(
        functools.partial(update_kernel, groups),
        grid=(front.shape[0],),
        out_shape=jax.ShapeDtypeStruct(front.shape, jnp.float32),
        in_specs=[
            SMEM,
            SMEM,
            tile,
            pl.BlockSpec((4, 1, 2, CHUNK, n), lambda c: (0, c, 0, 0, 0)),
            pl.BlockSpec((N, n), lambda c: (0, 0)),
            square,
            square,
        ],
        out_specs=tile,
        scratch_shapes=[pltpu.VMEM((N, n), jnp.float32)],
        name="schur_update",
    )(place, block_map, front, cols, rows, low, inv)


def device(z, y, x, core):
    return ((z % 8 * 4 + y % 4) * 4 + x % 4) * 2 + core


Y_GROUPS = [[z * 4 + y for y in range(4)] for z in range(8)]
Z_GROUPS = [[z * 4 + y for z in range(8)] for y in range(4)]
XS, YS, ZS = range(4), range(4), range(8)


def gather(value, axis, size, groups=None):
    return lax.all_to_all(jnp.broadcast_to(value, (size, *value.shape)), axis, 0, 0, axis_index_groups=groups)


def send(value, pairs):
    return lax.ppermute(value, BOTH, pairs)


def receive(value, arrived):
    for hit, got in arrived:
        value = jnp.where(hit, got, value)
    return value


def run(groups, front, block_map):
    p = lax.axis_index("row")
    q = lax.axis_index("col")
    z, y, x, core = p // 4, p % 4, q // 2, q % 2
    place = jnp.stack([p, q]).astype(jnp.int32)
    *sent, panel = prepare(groups, place, block_map, front)
    shares, chunks = sent[:4], sent[4:]

    arrived = [(x == d, send(shares[d], [(device(0, 0, 0, 0), device(0, 0, d, 0))])) for d in (1, 3, 2)]
    share = receive(shares[0], arrived)
    pieces = [send(chunks[t], [(s * 8, (s // 8 * 8 + t) * 8 + s % 8) for s in range(32)]) for t in range(8)]
    arrived = [
        (y == d, send(share, [(device(0, 0, i, 0), device(0, d, i, 0)) for i in XS])) for d in (1, 3, 2)
    ]
    share = receive(share, arrived)
    arrived = [(z == 4, send(share, [(device(0, j, i, 0), device(4, j, i, 0)) for j in YS for i in XS]))]
    share = receive(share, arrived)
    arrived = [
        (z % 4 == d % 4, send(share, [(device(k, j, i, 0), device(k + d, j, i, 0)) for k in (0, 4) for j in YS for i in XS]))
        for d in (1, 7, 2)
    ]
    share = receive(share, arrived)
    piece = receive(pieces[0], [(p % 8 == t, pieces[t]) for t in range(1, 8)])
    cols = gather(gather(piece, "row", 8, Z_GROUPS), "row", 4, Y_GROUPS).reshape(4, 4, 2, CHUNK, N // groups)
    quarters = [share] + [
        send(share, [(device(k, j, i + d, 0), device(k, j, i, 0)) for k in ZS for j in YS for i in XS]) for d in (1, 3, 2)
    ]
    swap = [(device(k, j, i, 0), device(k, j, i, 1)) for k in ZS for j in YS for i in XS]
    quarters = [jnp.where(core == 1, send(one, swap), one) for one in quarters]
    arrived = [
        (x == d, send(panel, [(device(k, j, 0, 0), device(k, j, d, 0)) for k in ZS for j in YS])) for d in (1, 3, 2)
    ]
    row = receive(panel, arrived)
    row = jnp.where(core == 1, send(row, swap), row)

    low, inv = pivot(groups, place, quarters)
    return update(groups, place, block_map, front, cols, row, low, inv)


def body(front_matrix, block_map):
    front = front_matrix[0, 0, :, 0]
    out = lax.cond(
        block_map[0, 1] != 0,
        functools.partial(run, 1),
        functools.partial(run, 2),
        front,
        block_map,
    )
    return out.reshape(front_matrix.shape)


def solution(mesh):
    return jax.shard_map(
        body,
        mesh=mesh,
        in_specs=(P(None, "row", None, "col", None, None), P()),
        out_specs=P(None, "row", None, "col", None, None),
        check_vma=False,
    )
```

```python
import functools

import jax
import jax.numpy as jnp
from jax import lax
from jax.experimental import pallas as pl
from jax.experimental.pallas import tpu as pltpu
from jax.sharding import PartitionSpec as P

BS = 256
N = 512
NB = 128
CHUNK = N // 8
AROUND = (0, 1, 3, 2)
HIGHEST = lax.Precision.HIGHEST
BOTH = ("row", "col")
VMEM = pl.BlockSpec(memory_space=pltpu.VMEM)
SMEM = pl.BlockSpec(memory_space=pltpu.SMEM)


def dot_nn(a, b):
    return lax.dot_general(a, b, (((1,), (0,)), ((), ())), precision=HIGHEST, preferred_element_type=jnp.float32)


def dot_nt(a, b):
    return lax.dot_general(a, b, (((1,), (1,)), ((), ())), precision=HIGHEST, preferred_element_type=jnp.float32)


def spread(row):
    return jnp.broadcast_to(row, (8, NB))


def factor_blocks(d_refs, m_refs):
    sub = lax.broadcasted_iota(jnp.int32, (8, NB), 0)
    lane = lax.broadcasted_iota(jnp.int32, (8, NB), 1)
    for first in range(0, NB, 32):
        tiles_of = [[d_ref[first + 8 * t : first + 8 * t + 8, :] for t in range(4)] for d_ref in d_refs]
        for step in range(4):
            s = first + 8 * step
            here = (lane >= s) & (lane < s + 8)
            state = []
            for tiles in tiles_of:
                cols = [spread(tiles[step][:, s + k : s + k + 1]) for k in range(8)]
                rows = jnp.where(here, jnp.where(lane == sub + s, 1.0, 0.0), tiles[step])
                state.append([cols, rows, jnp.ones_like(rows), rows])
            for j in range(8):
                own = sub == j
                for one in state:
                    cols, rows, diag, kept = one
                    d = cols[j][j : j + 1, :]
                    diag = jnp.where(own, spread(d), diag)
                    factor = jnp.where(own, 0.0, cols[j] * spread(1.0 / d))
                    for k in range(j + 1, 8):
                        cols[k] = cols[k] - factor * spread(cols[k][j : j + 1, :])
                    pivot_row = spread(rows[j : j + 1, :])
                    one[1:] = rows - factor * pivot_row, diag, jnp.where(own, pivot_row, kept)
            for tiles, m_ref, (_, rows, diag, kept) in zip(tiles_of, m_refs, state):
                m_ref[s : s + 8, :] = jnp.where(lane < s + 8, kept * lax.rsqrt(diag), 0.0)
                tiles[step] = rows / diag
                solved = [spread(tiles[step][k : k + 1, :]) for k in range(8)]
                for t in [*range(step + 1, 4), *range(step)]:
                    old = tiles[t]
                    terms = [spread(old[:, s + k : s + k + 1]) * solved[k] for k in range(8)]
                    while len(terms) > 1:
                        terms = [a + b for a, b in zip(terms[::2], terms[1::2])]
                    tiles[t] = jnp.where(here, 0.0, old) - terms[0]
        if first + 32 < NB:
            for tiles, d_ref in zip(tiles_of, d_refs):
                below = d_ref[first + 32 :, :]
                above = [jnp.zeros((first, NB), jnp.float32)] if first else []
                under = [jnp.zeros((NB - first - 32, NB), jnp.float32)]
                column = lax.broadcasted_iota(jnp.int32, below.shape, 1)
                inside = (column >= first) & (column < first + 32)
                product = dot_nn(below, jnp.concatenate(above + tiles + under, axis=0))
                d_ref[first + 32 :, :] = jnp.where(inside, 0.0, below) - product


def panels(groups):
    out, at = [], 0
    for b in range(N // groups // NB):
        for g in range(groups):
            height = N // groups - b * NB
            out.append((g, b, at, height))
            at += height
    return out


def packed_rows(groups):
    return sum(height for _, _, _, height in panels(groups))


def gathered(place_ref, near_refs, far_ref):
    x, core = place_ref[1] // 2, place_ref[1] % 2
    height = near_refs[0].shape[0]
    for at, (step, ref) in enumerate(zip(AROUND, near_refs)):
        there = lax.rem(x + step, 4) * 2
        yield there + core, ref
        yield there + 1 - core, far_ref.at[at * height : (at + 1) * height, :]


def pivot_kernel(groups, place_ref, *refs):
    near_refs, (far_ref, l_ref, inv_ref, w_ref, x_ref, d_ref, m_ref) = refs[:4], refs[4:]
    n = N // groups
    share, rows = packed_rows(groups) // 8, pivot_rows(groups)
    for col, ref in gathered(place_ref, near_refs, far_ref):
        for b in range(n // NB):
            here = pl.ds(pl.multiple_of(col * share + b * rows, 8), rows)
            w_ref[here, :] = ref[:rows, b * NB : (b + 1) * NB]
    starts = {(g, b): (at, height) for g, b, at, height in panels(groups)}
    row_ids = lax.broadcasted_iota(jnp.int32, (n, n), 0)
    col_ids = lax.broadcasted_iota(jnp.int32, (n, n), 1)
    for g in range(groups):
        x_ref[g] = jnp.where(row_ids == col_ids, 1.0, 0.0).astype(jnp.float32)
    for b in range(n // NB):
        o, e = b * NB, (b + 1) * NB
        for g in range(groups):
            d_ref[g] = w_ref[pl.ds(starts[g, b][0], NB), :]
        factor_blocks([d_ref.at[g] for g in range(groups)], [m_ref.at[g] for g in range(groups)])
        for g in range(groups):
            at, height = starts[g, b]
            m = m_ref[g]
            low = dot_nt(w_ref[at : at + height, :], m)
            if e < n:
                for k in range(b + 1, n // NB):
                    rest = low[(k - b) * NB :]
                    to, tall = starts[g, k]
                    w_ref[to : to + tall, :] -= dot_nt(rest, rest[:NB])
            tri = lax.broadcasted_iota(jnp.int32, low.shape, 0) >= lax.broadcasted_iota(jnp.int32, low.shape, 1)
            l_ref[g, o:, o:e] = jnp.where(tri, low, 0.0)
            inv = dot_nn(m, x_ref[g, o:e, :e])
            inv_ref[g, o:e, :e] = inv
            if b:
                l_ref[g, :o, o:e] = jnp.zeros((o, NB), jnp.float32)
            if e < n:
                inv_ref[g, o:e, e:] = jnp.zeros((NB, n - e), jnp.float32)
                x_ref[g, e:, :e] -= dot_nn(low[NB:], inv)


def pivot(groups, place, near, far):
    n = N // groups
    return pl.pallas_call(
        functools.partial(pivot_kernel, groups),
        out_shape=(jax.ShapeDtypeStruct((groups, n, n), jnp.float32),) * 2,
        in_specs=[SMEM] + [VMEM] * 5,
        out_specs=(VMEM, VMEM),
        scratch_shapes=[
            pltpu.VMEM((packed_rows(groups), NB), jnp.float32),
            pltpu.VMEM((groups, n, n), jnp.float32),
            pltpu.VMEM((groups, NB, NB), jnp.float32),
            pltpu.VMEM((groups, NB, NB), jnp.float32),
        ],
        name="pivot_cholesky",
    )(place, *near, far)


def pivot_rows(groups):
    return packed_rows(groups) // 8 * NB * groups // N


def prepare_kernel(groups, place_ref, map_ref, head_ref, out_ref):
    p = place_ref[0]
    n = N // groups

    @pl.when(p > 0)
    def _():
        for a in range(2):
            rows = slice(a * BS, (a + 1) * BS)
            panel = head_ref[0, rows, :n] * map_ref[2 * p + a, 0].astype(jnp.float32)
            if groups == 2:
                panel = panel + head_ref[0, rows, n:] * map_ref[2 * p + a, 1].astype(jnp.float32)
            for t in range(4):
                out_ref[4 * a + t] = panel[t * CHUNK : (t + 1) * CHUNK]

    @pl.when(p == 0)
    def _():
        lower = []
        for g, b, _, height in panels(groups):
            first = g * n + b * NB
            lower.append(head_ref[0, first : first + height, first : first + NB])
        lower = jnp.concatenate(lower, axis=0)
        share, rows = packed_rows(groups) // 8, pivot_rows(groups)
        for t in range(8):
            for b in range(n // NB):
                first = t * share + b * rows
                out_ref[t, :rows, b * NB : (b + 1) * NB] = lower[first : first + rows]
            out_ref[t, rows:, :] = jnp.zeros((CHUNK - rows, n), jnp.float32)


def prepare(groups, place, block_map, front):
    shape = (8, CHUNK, N // groups)
    return pl.pallas_call(
        functools.partial(prepare_kernel, groups),
        grid=(1,),
        out_shape=jax.ShapeDtypeStruct(shape, jnp.float32),
        in_specs=[SMEM, SMEM, pl.BlockSpec((1, N, N), lambda i: (0, 0, 0))],
        out_specs=pl.BlockSpec(shape, lambda i: (0, 0, 0)),
        name="prepare",
    )(place, block_map, front)


def update_kernel(groups, place_ref, map_ref, front_ref, col_ref, *refs):
    near_refs, (far_ref, l_ref, inv_ref, out_ref, row_ref, row_factor_ref) = refs[:4], refs[4:]
    c = pl.program_id(0)
    p, q = place_ref[0], place_ref[1]
    j = c * 8 + q
    n = N // groups

    def marked(r, s):
        return map_ref[r, s] != 0

    def in_panel(r):
        return marked(r, 0) | marked(r, 1)

    def inverse(r):
        return inv_ref[map_ref[r, 1]] if groups == 2 else inv_ref[0]

    @pl.when(c == 0)
    def _():
        for col, ref in gathered(place_ref, near_refs, far_ref):
            row_ref[pl.ds(pl.multiple_of(col * CHUNK, 8), CHUNK), :] = ref[pivot_rows(groups) :, :]
        for a in range(2):
            rows = slice(a * BS, (a + 1) * BS)
            row_factor_ref[rows, :] = dot_nt(row_ref[rows, :], inverse(2 * p + a))

    @pl.when((p > 0) & (j > 0))
    def _():
        for b in range(2):
            s = 2 * j + b
            cols = slice(b * BS, (b + 1) * BS)
            touched = [marked(2 * p + a, s) & in_panel(s) for a in range(2)]

            @pl.when(touched[0] | touched[1])
            def _():
                block = jnp.concatenate([col_ref[t, 0, b] for t in range(4)], axis=0)
                factor = dot_nt(block, inverse(s))
                for a in range(2):

                    @pl.when(touched[a])
                    def _():
                        rows = slice(a * BS, (a + 1) * BS)
                        out_ref[0, rows, cols] = front_ref[0, rows, cols] - dot_nt(row_factor_ref[rows, :], factor)

            for a in range(2):

                @pl.when(jnp.logical_not(touched[a]))
                def _():
                    rows = slice(a * BS, (a + 1) * BS)
                    weight = map_ref[2 * p + a, s].astype(jnp.float32)
                    out_ref[0, rows, cols] = front_ref[0, rows, cols] * weight

    @pl.when((p > 0) & (j == 0))
    def _():
        for a in range(2):
            rows = slice(a * BS, (a + 1) * BS)
            if groups == 1:
                out_ref[0, rows, :] = row_factor_ref[rows, :]
            else:
                for b in range(2):
                    weight = map_ref[2 * p + a, b].astype(jnp.float32)
                    out_ref[0, rows, b * BS : (b + 1) * BS] = row_factor_ref[rows, :] * weight

    @pl.when((p == 0) & (j > 0))
    def _():
        out_ref[0] = jnp.zeros((N, N), jnp.float32)

    @pl.when((p == 0) & (j == 0))
    def _():
        out_ref[0] = jnp.zeros((N, N), jnp.float32)
        for g in range(groups):
            out_ref[0, g * n : (g + 1) * n, g * n : (g + 1) * n] = l_ref[g]


def update(groups, place, block_map, front, cols, near, far, low, inv):
    n = N // groups
    tile = pl.BlockSpec((1, N, N), lambda c: (c, 0, 0))
    square = pl.BlockSpec((groups, n, n), lambda c: (0, 0, 0))
    return pl.pallas_call(
        functools.partial(update_kernel, groups),
        grid=(front.shape[0],),
        out_shape=jax.ShapeDtypeStruct(front.shape, jnp.float32),
        in_specs=[
            SMEM,
            SMEM,
            tile,
            pl.BlockSpec((4, 1, 2, CHUNK, n), lambda c: (0, c, 0, 0, 0)),
            *[pl.BlockSpec(one.shape, lambda c: (0, 0)) for one in (*near, far)],
            square,
            square,
        ],
        out_specs=tile,
        scratch_shapes=[pltpu.VMEM((N, n), jnp.float32), pltpu.VMEM((N, n), jnp.float32)],
        name="schur_update",
    )(place, block_map, front, cols, *near, far, low, inv)


def device(z, y, x, core):
    return ((z % 8 * 4 + y % 4) * 4 + x % 4) * 2 + core


Y_GROUPS = [[z * 4 + y for y in range(4)] for z in range(8)]
Z_GROUPS = [[z * 4 + y for z in range(8)] for y in range(4)]
XS, YS, ZS = range(4), range(4), range(8)


def gather(value, axis, size, groups=None):
    return lax.all_to_all(jnp.broadcast_to(value, (size, *value.shape)), axis, 0, 0, axis_index_groups=groups)


def send(value, pairs):
    return lax.ppermute(value, BOTH, pairs)


def receive(value, arrived):
    for hit, got in arrived:
        value = jnp.where(hit, got, value)
    return value


def run(groups, front, block_map):
    p = lax.axis_index("row")
    q = lax.axis_index("col")
    z, y = p // 4, p % 4
    place = jnp.stack([p, q]).astype(jnp.int32)
    lanes = [(i, k) for i in XS for k in range(2)]
    every = [(k, j, *lane) for k in ZS for j in YS for lane in lanes]

    eighth = lax.all_to_all(prepare(groups, place, block_map, front), "col", 0, 0)[0]
    share = eighth[: pivot_rows(groups)]
    piece = send(eighth, [((s // 8 * 8 + a) * 8 + b, (s // 8 * 8 + b) * 8 + a) for s in range(0, 32, 8) for a in range(8) for b in range(8)])
    arrived = [(z == 4, send(share, [(device(0, 0, *lane), device(4, 0, *lane)) for lane in lanes]))]
    share = receive(share, arrived)
    share, piece = lax.optimization_barrier((share, piece))
    arrived = [
        (z % 4 == d % 4, send(share, [(device(k, 0, *lane), device(k + d, 0, *lane)) for k in (0, 4) for lane in lanes]))
        for d in (1, 7, 2)
    ]
    share = receive(share, arrived)
    arrived = [(y == d, send(share, [(device(k, 0, *lane), device(k, d, *lane)) for k in ZS for lane in lanes])) for d in (1, 3, 2)]
    share = receive(share, arrived)
    cols = gather(piece, "row", 8, Z_GROUPS)
    share, cols = lax.optimization_barrier((share, cols))
    cols = gather(cols, "row", 4, Y_GROUPS).reshape(4, 4, 2, CHUNK, N // groups)
    near = [jnp.concatenate([share, eighth], axis=0)]
    near += [send(near[0], [(device(k, j, i + d, c), device(k, j, i, c)) for k, j, i, c in every]) for d in AROUND[1:]]
    far = send(jnp.concatenate(near, axis=0), [(device(k, j, i, c), device(k, j, i, 1 - c)) for k, j, i, c in every])

    low, inv = pivot(groups, place, near, far)
    return update(groups, place, block_map, front, cols, near, far, low, inv)


def body(front_matrix, block_map):
    front = front_matrix[0, 0, :, 0]
    out = lax.cond(
        block_map[0, 1] != 0,
        functools.partial(run, 1),
        functools.partial(run, 2),
        front,
        block_map,
    )
    return out.reshape(front_matrix.shape)


def solution(mesh):
    return jax.shard_map(
        body,
        mesh=mesh,
        in_specs=(P(None, "row", None, "col", None, None), P()),
        out_specs=P(None, "row", None, "col", None, None),
        check_vma=False,
    )
```

```python
import functools

import jax
import jax.numpy as jnp
from jax import lax
from jax.experimental import pallas as pl
from jax.experimental.pallas import tpu as pltpu
from jax.sharding import PartitionSpec as P

BS = 256
N = 512
NB = 128
CHUNK = N // 8
AROUND = (0, 1, 3, 2)
HIGHEST = lax.Precision.HIGHEST
BOTH = ("row", "col")
VMEM = pl.BlockSpec(memory_space=pltpu.VMEM)
SMEM = pl.BlockSpec(memory_space=pltpu.SMEM)


def dot_nn(a, b):
    return lax.dot_general(a, b, (((1,), (0,)), ((), ())), precision=HIGHEST, preferred_element_type=jnp.float32)


def dot_nt(a, b):
    return lax.dot_general(a, b, (((1,), (1,)), ((), ())), precision=HIGHEST, preferred_element_type=jnp.float32)


def spread(row):
    return jnp.broadcast_to(row, (8, NB))


def factor_blocks(d_refs, m_refs):
    sub = lax.broadcasted_iota(jnp.int32, (8, NB), 0)
    lane = lax.broadcasted_iota(jnp.int32, (8, NB), 1)
    for first in range(0, NB, 32):
        tiles_of = [[d_ref[first + 8 * t : first + 8 * t + 8, :] for t in range(4)] for d_ref in d_refs]
        for step in range(4):
            s = first + 8 * step
            here = (lane >= s) & (lane < s + 8)
            state = []
            for tiles in tiles_of:
                cols = [spread(tiles[step][:, s + k : s + k + 1]) for k in range(8)]
                rows = jnp.where(here, jnp.where(lane == sub + s, 1.0, 0.0), tiles[step])
                state.append([cols, rows, jnp.ones_like(rows), rows])
            for j in range(8):
                own = sub == j
                for one in state:
                    cols, rows, diag, kept = one
                    d = cols[j][j : j + 1, :]
                    diag = jnp.where(own, spread(d), diag)
                    factor = jnp.where(own, 0.0, cols[j] * spread(1.0 / d))
                    for k in range(j + 1, 8):
                        cols[k] = cols[k] - factor * spread(cols[k][j : j + 1, :])
                    pivot_row = spread(rows[j : j + 1, :])
                    one[1:] = rows - factor * pivot_row, diag, jnp.where(own, pivot_row, kept)
            for tiles, m_ref, (_, rows, diag, kept) in zip(tiles_of, m_refs, state):
                m_ref[s : s + 8, :] = jnp.where(lane < s + 8, kept * lax.rsqrt(diag), 0.0)
                tiles[step] = rows / diag
                solved = [spread(tiles[step][k : k + 1, :]) for k in range(8)]
                for t in [*range(step + 1, 4), *range(step)]:
                    old = tiles[t]
                    terms = [spread(old[:, s + k : s + k + 1]) * solved[k] for k in range(8)]
                    while len(terms) > 1:
                        terms = [a + b for a, b in zip(terms[::2], terms[1::2])]
                    tiles[t] = jnp.where(here, 0.0, old) - terms[0]
        if first + 32 < NB:
            for tiles, d_ref in zip(tiles_of, d_refs):
                below = d_ref[first + 32 :, :]
                above = [jnp.zeros((first, NB), jnp.float32)] if first else []
                under = [jnp.zeros((NB - first - 32, NB), jnp.float32)]
                column = lax.broadcasted_iota(jnp.int32, below.shape, 1)
                inside = (column >= first) & (column < first + 32)
                product = dot_nn(below, jnp.concatenate(above + tiles + under, axis=0))
                d_ref[first + 32 :, :] = jnp.where(inside, 0.0, below) - product


def panels(groups):
    out, at = [], 0
    for b in range(N // groups // NB):
        for g in range(groups):
            height = N // groups - b * NB
            out.append((g, b, at, height))
            at += height
    return out


def packed_rows(groups):
    return sum(height for _, _, _, height in panels(groups))


def gathered(place_ref, near_refs, far_ref):
    x, core = place_ref[1] // 2, place_ref[1] % 2
    height = near_refs[0].shape[0]
    for at, (step, ref) in enumerate(zip(AROUND, near_refs)):
        there = lax.rem(x + step, 4) * 2
        yield there + core, ref
        yield there + 1 - core, far_ref.at[at * height : (at + 1) * height, :]


def pivot_kernel(groups, place_ref, *refs):
    near_refs, (far_ref, l_ref, inv_ref, w_ref, x_ref, d_ref, m_ref) = refs[:4], refs[4:]
    n = N // groups
    share, rows = packed_rows(groups) // 8, pivot_rows(groups)
    for col, ref in gathered(place_ref, near_refs, far_ref):
        for b in range(n // NB):
            here = pl.ds(pl.multiple_of(col * share + b * rows, 8), rows)
            w_ref[here, :] = ref[:rows, b * NB : (b + 1) * NB]
    starts = {(g, b): (at, height) for g, b, at, height in panels(groups)}
    row_ids = lax.broadcasted_iota(jnp.int32, (n, n), 0)
    col_ids = lax.broadcasted_iota(jnp.int32, (n, n), 1)
    for g in range(groups):
        x_ref[g] = jnp.where(row_ids == col_ids, 1.0, 0.0).astype(jnp.float32)
    for b in range(n // NB):
        o, e = b * NB, (b + 1) * NB
        for g in range(groups):
            d_ref[g] = w_ref[pl.ds(starts[g, b][0], NB), :]
        factor_blocks([d_ref.at[g] for g in range(groups)], [m_ref.at[g] for g in range(groups)])
        for g in range(groups):
            at, height = starts[g, b]
            m = m_ref[g]
            low = dot_nt(w_ref[at : at + height, :], m)
            if e < n:
                for k in range(b + 1, n // NB):
                    rest = low[(k - b) * NB :]
                    to, tall = starts[g, k]
                    w_ref[to : to + tall, :] -= dot_nt(rest, rest[:NB])
            tri = lax.broadcasted_iota(jnp.int32, low.shape, 0) >= lax.broadcasted_iota(jnp.int32, low.shape, 1)
            l_ref[g, o:, o:e] = jnp.where(tri, low, 0.0)
            inv = dot_nn(m, x_ref[g, o:e, :e])
            inv_ref[g, o:e, :e] = inv
            if b:
                l_ref[g, :o, o:e] = jnp.zeros((o, NB), jnp.float32)
            if e < n:
                inv_ref[g, o:e, e:] = jnp.zeros((NB, n - e), jnp.float32)
                x_ref[g, e:, :e] -= dot_nn(low[NB:], inv)


def pivot(groups, place, near, far):
    n = N // groups
    return pl.pallas_call(
        functools.partial(pivot_kernel, groups),
        out_shape=(jax.ShapeDtypeStruct((groups, n, n), jnp.float32),) * 2,
        in_specs=[SMEM] + [VMEM] * 5,
        out_specs=(VMEM, VMEM),
        scratch_shapes=[
            pltpu.VMEM((packed_rows(groups), NB), jnp.float32),
            pltpu.VMEM((groups, n, n), jnp.float32),
            pltpu.VMEM((groups, NB, NB), jnp.float32),
            pltpu.VMEM((groups, NB, NB), jnp.float32),
        ],
        name="pivot_cholesky",
    )(place, *near, far)


def pivot_rows(groups):
    return packed_rows(groups) // 8 * NB * groups // N


def prepare_kernel(groups, place_ref, map_ref, head_ref, out_ref):
    p = place_ref[0]
    n = N // groups

    @pl.when(p > 0)
    def _():
        for a in range(2):
            rows = slice(a * BS, (a + 1) * BS)
            panel = head_ref[0, rows, :n] * map_ref[2 * p + a, 0].astype(jnp.float32)
            if groups == 2:
                panel = panel + head_ref[0, rows, n:] * map_ref[2 * p + a, 1].astype(jnp.float32)
            for t in range(4):
                out_ref[4 * a + t] = panel[t * CHUNK : (t + 1) * CHUNK]

    @pl.when(p == 0)
    def _():
        lower = []
        for g, b, _, height in panels(groups):
            first = g * n + b * NB
            lower.append(head_ref[0, first : first + height, first : first + NB])
        lower = jnp.concatenate(lower, axis=0)
        share, rows = packed_rows(groups) // 8, pivot_rows(groups)
        for t in range(8):
            for b in range(n // NB):
                first = t * share + b * rows
                out_ref[t, :rows, b * NB : (b + 1) * NB] = lower[first : first + rows]
            out_ref[t, rows:, :] = jnp.zeros((CHUNK - rows, n), jnp.float32)


def prepare(groups, place, block_map, front):
    shape = (8, CHUNK, N // groups)
    return pl.pallas_call(
        functools.partial(prepare_kernel, groups),
        grid=(1,),
        out_shape=jax.ShapeDtypeStruct(shape, jnp.float32),
        in_specs=[SMEM, SMEM, pl.BlockSpec((1, N, N), lambda i: (0, 0, 0))],
        out_specs=pl.BlockSpec(shape, lambda i: (0, 0, 0)),
        name="prepare",
    )(place, block_map, front)


def split(value, parts):
    out = []
    for _ in range(parts):
        out.append(value.astype(jnp.bfloat16))
        value = value - out[-1].astype(jnp.float32)
    return out


def split_dot_nt(left, right):
    total = None
    for rank in reversed(range(len(left))):
        for i in range(rank + 1):
            one = lax.dot_general(
                left[i], right[rank - i], (((1,), (1,)), ((), ())), preferred_element_type=jnp.float32
            )
            total = one if total is None else total + one
    return total


def update_kernel(groups, place_ref, map_ref, front_ref, col_ref, *refs):
    near_refs, (far_ref, l_ref, inv_ref, out_ref, row_ref, inv_parts_ref, row_parts_ref) = refs[:4], refs[4:]
    c = pl.program_id(0)
    p, q = place_ref[0], place_ref[1]
    j = c * 8 + q
    n = N // groups

    def marked(r, s):
        return map_ref[r, s] != 0

    def in_panel(r):
        return marked(r, 0) | marked(r, 1)

    def solve(block, r):
        group = map_ref[r, 1] if groups == 2 else 0
        return split_dot_nt(split(block, 3), [inv_parts_ref[k, group] for k in range(3)])

    @pl.when(c == 0)
    def _():
        for g in range(groups):
            for k, part in enumerate(split(inv_ref[g], 3)):
                inv_parts_ref[k, g] = part
        for col, ref in gathered(place_ref, near_refs, far_ref):
            row_ref[pl.ds(pl.multiple_of(col * CHUNK, 8), CHUNK), :] = ref[pivot_rows(groups) :, :]
        for a in range(2):
            rows = slice(a * BS, (a + 1) * BS)
            factor = solve(row_ref[rows, :], 2 * p + a)
            row_ref[rows, :] = factor
            for k, part in enumerate(split(factor, 2)):
                row_parts_ref[k, rows, :] = part

    @pl.when((p > 0) & (j > 0))
    def _():
        for b in range(2):
            s = 2 * j + b
            cols = slice(b * BS, (b + 1) * BS)
            touched = [marked(2 * p + a, s) & in_panel(s) for a in range(2)]

            @pl.when(touched[0] | touched[1])
            def _():
                block = jnp.concatenate([col_ref[t, 0, b] for t in range(4)], axis=0)
                factor = split(solve(block, s), 2)
                for a in range(2):

                    @pl.when(touched[a])
                    def _():
                        rows = slice(a * BS, (a + 1) * BS)
                        product = split_dot_nt([row_parts_ref[k, rows, :] for k in range(2)], factor)
                        out_ref[0, rows, cols] = front_ref[0, rows, cols] - product

            for a in range(2):

                @pl.when(jnp.logical_not(touched[a]))
                def _():
                    rows = slice(a * BS, (a + 1) * BS)
                    weight = map_ref[2 * p + a, s].astype(jnp.float32)
                    out_ref[0, rows, cols] = front_ref[0, rows, cols] * weight

    @pl.when((p > 0) & (j == 0))
    def _():
        for a in range(2):
            rows = slice(a * BS, (a + 1) * BS)
            if groups == 1:
                out_ref[0, rows, :] = row_ref[rows, :]
            else:
                for b in range(2):
                    weight = map_ref[2 * p + a, b].astype(jnp.float32)
                    out_ref[0, rows, b * BS : (b + 1) * BS] = row_ref[rows, :] * weight

    @pl.when((p == 0) & (j > 0))
    def _():
        out_ref[0] = jnp.zeros((N, N), jnp.float32)

    @pl.when((p == 0) & (j == 0))
    def _():
        out_ref[0] = jnp.zeros((N, N), jnp.float32)
        for g in range(groups):
            out_ref[0, g * n : (g + 1) * n, g * n : (g + 1) * n] = l_ref[g]


def update(groups, place, block_map, front, cols, near, far, low, inv):
    n = N // groups
    tile = pl.BlockSpec((1, N, N), lambda c: (c, 0, 0))
    square = pl.BlockSpec((groups, n, n), lambda c: (0, 0, 0))
    return pl.pallas_call(
        functools.partial(update_kernel, groups),
        grid=(front.shape[0],),
        out_shape=jax.ShapeDtypeStruct(front.shape, jnp.float32),
        in_specs=[
            SMEM,
            SMEM,
            tile,
            pl.BlockSpec((4, 1, 2, CHUNK, n), lambda c: (0, c, 0, 0, 0)),
            *[pl.BlockSpec(one.shape, lambda c: (0, 0)) for one in (*near, far)],
            square,
            square,
        ],
        out_specs=tile,
        scratch_shapes=[
            pltpu.VMEM((N, n), jnp.float32),
            pltpu.VMEM((3, groups, n, n), jnp.bfloat16),
            pltpu.VMEM((2, N, n), jnp.bfloat16),
        ],
        name="schur_update",
    )(place, block_map, front, cols, *near, far, low, inv)


def device(z, y, x, core):
    return ((z % 8 * 4 + y % 4) * 4 + x % 4) * 2 + core


Y_GROUPS = [[z * 4 + y for y in range(4)] for z in range(8)]
Z_GROUPS = [[z * 4 + y for z in range(8)] for y in range(4)]
XS, YS, ZS = range(4), range(4), range(8)


def gather(value, axis, size, groups=None):
    return lax.all_to_all(jnp.broadcast_to(value, (size, *value.shape)), axis, 0, 0, axis_index_groups=groups)


def send(value, pairs):
    return lax.ppermute(value, BOTH, pairs)


def receive(value, arrived):
    for hit, got in arrived:
        value = jnp.where(hit, got, value)
    return value


def run(groups, front, block_map):
    p = lax.axis_index("row")
    q = lax.axis_index("col")
    z, y = p // 4, p % 4
    place = jnp.stack([p, q]).astype(jnp.int32)
    lanes = [(i, k) for i in XS for k in range(2)]
    every = [(k, j, *lane) for k in ZS for j in YS for lane in lanes]

    eighth = lax.all_to_all(prepare(groups, place, block_map, front), "col", 0, 0)[0]
    share = eighth[: pivot_rows(groups)]
    piece = send(eighth, [((s // 8 * 8 + a) * 8 + b, (s // 8 * 8 + b) * 8 + a) for s in range(0, 32, 8) for a in range(8) for b in range(8)])
    arrived = [(z == 4, send(share, [(device(0, 0, *lane), device(4, 0, *lane)) for lane in lanes]))]
    share = receive(share, arrived)
    share, piece = lax.optimization_barrier((share, piece))
    arrived = [
        (z % 4 == d % 4, send(share, [(device(k, 0, *lane), device(k + d, 0, *lane)) for k in (0, 4) for lane in lanes]))
        for d in (1, 7, 2)
    ]
    share = receive(share, arrived)
    arrived = [(y == d, send(share, [(device(k, 0, *lane), device(k, d, *lane)) for k in ZS for lane in lanes])) for d in (1, 3, 2)]
    share = receive(share, arrived)
    cols = gather(piece, "row", 8, Z_GROUPS)
    share, cols = lax.optimization_barrier((share, cols))
    cols = gather(cols, "row", 4, Y_GROUPS).reshape(4, 4, 2, CHUNK, N // groups)
    near = [jnp.concatenate([share, eighth], axis=0)]
    near += [send(near[0], [(device(k, j, i + d, c), device(k, j, i, c)) for k, j, i, c in every]) for d in AROUND[1:]]
    far = send(jnp.concatenate(near, axis=0), [(device(k, j, i, c), device(k, j, i, 1 - c)) for k, j, i, c in every])

    low, inv = pivot(groups, place, near, far)
    return update(groups, place, block_map, front, cols, near, far, low, inv)


def body(front_matrix, block_map):
    front = front_matrix[0, 0, :, 0]
    out = lax.cond(
        block_map[0, 1] != 0,
        functools.partial(run, 1),
        functools.partial(run, 2),
        front,
        block_map,
    )
    return out.reshape(front_matrix.shape)


def solution(mesh):
    return jax.shard_map(
        body,
        mesh=mesh,
        in_specs=(P(None, "row", None, "col", None, None), P()),
        out_specs=P(None, "row", None, "col", None, None),
        check_vma=False,
    )
```
